512 devices in a mesh: mp: 32 (over z, y_lo), dp: 16 (over x, y_hi, core).
Axes of the slice: x: 4, y: 4 (y_hi: 2, y_lo: 2; y = y_hi * 2 + y_lo), z: 16, core: 2. Of those that a mesh axis runs over, the one named last changes fastest.
Arguments:
- inputs: bfloat16 [256, 8192], P('mp', 'dp'), may hold values from -6 to 6
- w_up: bfloat16 [8192, 32768], P('dp', 'mp'), may hold values from -0.0625 to 0.0625
- w_down: bfloat16 [32768, 8192], P('mp', 'dp'), may hold values from -0.03125 to 0.03125
- cotangent: bfloat16 [256, 8192], P('mp', 'dp'), may hold values from -6 to 6
Outputs:
- output: bfloat16 [256, 8192], P('mp', 'dp')
- grad_inputs: bfloat16 [256, 8192], P('mp', 'dp')
- grad_up: bfloat16 [8192, 32768], P('dp', 'mp')
- grad_down: bfloat16 [32768, 8192], P('mp', 'dp')
The draws below stay inside these ranges and needn't reach their ends.
All inputs are finite; a program needn't handle non-finite values.
Results may differ from the reference program's by a relative error of at most 0.0049.
Values may be sent and summed in bfloat16 or wider, within the bound.
No kernel may reach another device: no remote copies, remote signals or barrier semaphores. Data moves between devices by JAX's collectives and lax.ppermute only.
A program may use at most 64 MiB of HBM per device.

```python
import jax
import jax.numpy as jnp

D = 8192
FF = 32768
TOKENS = 256


def levels(key, shape, cuts, smallest, largest):
    def one(axis_at, parts):
        draws = jax.random.uniform(jax.random.fold_in(jax.random.fold_in(key, 6), axis_at), (parts,), jnp.float32, smallest / len(cuts), largest / len(cuts))
        return jnp.repeat(jnp.exp(draws), shape[axis_at] // parts).reshape((-1,) + (1,) * (len(shape) - axis_at - 1))

    level = one(*cuts[0])
    for cut in cuts[1:]:
        level = level * one(*cut)
    return level


def normal_values(rng, dims, width, reach, cuts=(), dtype=jnp.bfloat16):
    values = jax.random.normal(rng, dims, jnp.float32) * width
    if len(cuts) > 0:
        values = levels(rng, dims, cuts, -0.22, 0.18) * values
    return jnp.clip(values, min=-reach, max=reach).astype(dtype)


def setup_inputs(seed: int = 0) -> dict:
    arg_keys = jax.random.split(jax.random.key(seed), 5)
    inputs = normal_values(arg_keys[0], (TOKENS, D), 1.0, 6.0, ((0, 32), (1, 16)))
    w_up = normal_values(arg_keys[1], (D, FF), D ** -0.5, 0.0625, ((0, 16), (1, 32)))
    w_down = normal_values(arg_keys[2], (FF, D), FF ** -0.5, 0.03125, ((0, 32), (1, 16)))
    cotangent = normal_values(arg_keys[3], (TOKENS, D), 1.0, 6.0, ((0, 32), (1, 16)))
    return dict(inputs=inputs, w_up=w_up, w_down=w_down, cotangent=cotangent)


def gelu_tanh(values):
    return 0.5 * values * (1.0 + jnp.tanh(0.7978845608 * (values + 0.044715 * values * values * values)))

def reference(inputs, w_up, w_down, cotangent):
    hidden = jnp.dot(inputs, w_up, preferred_element_type=jnp.float32)
    activated = gelu_tanh(hidden).astype(jnp.bfloat16)
    output = jnp.dot(activated, w_down, preferred_element_type=jnp.float32).astype(jnp.bfloat16)
    grad_act = jnp.dot(cotangent, w_down.T, preferred_element_type=jnp.float32)
    unused, pullback = jax.vjp(gelu_tanh, hidden)
    grad_hidden = pullback(grad_act)[0].astype(jnp.bfloat16)
    grad_down = jnp.dot(activated.T, cotangent, preferred_element_type=jnp.float32).astype(jnp.bfloat16)
    grad_up = jnp.dot(inputs.T, grad_hidden, preferred_element_type=jnp.float32).astype(jnp.bfloat16)
    grad_inputs = jnp.dot(grad_hidden, w_up.T, preferred_element_type=jnp.float32).astype(jnp.bfloat16)
    return (output, grad_inputs, grad_up, grad_down)
```

```python
import jax
import jax.numpy as jnp
from jax import lax
from jax.sharding import Mesh
from jax.sharding import PartitionSpec as P

AXES = ("zh", "zl", "yl", "x", "yh", "core")
SIZES = (4, 4, 2, 4, 2, 2)
MP = ("zh", "zl", "yl")
DP = ("x", "yh", "core")
FAR = ("zh", "yl")
NEAR = "zl"
PLANE = ("x", "yh")
F32 = jnp.float32
BF16 = jnp.bfloat16


def gelu_tanh(values):
    return (
        0.5
        * values
        * (1.0 + jnp.tanh(0.7978845608 * (values + 0.044715 * values * values * values)))
    )


def gelu_back(hidden, grad_act):
    unused, pullback = jax.vjp(gelu_tanh, hidden)
    return pullback(grad_act)[0].astype(BF16)


def dot(a, b, ca, cb):
    return lax.dot_general(a, b, (((ca,), (cb,)), ((), ())), preferred_element_type=F32)


def spread(block, axes, count):
    copies = jnp.broadcast_to(block[None], (count,) + block.shape)
    return lax.all_to_all(copies, axes, 0, 0, tiled=True)


def swap(block):
    return lax.ppermute(block, "core", [(0, 1), (1, 0)])


def local(inputs, w_up, w_down, cotangent):
    core = lax.axis_index("core")
    pair = jnp.concatenate([inputs, cotangent], axis=1)
    far = spread(pair, FAR, 8).reshape(64, 1024)
    full = spread(far, NEAR, 4).reshape(256, 1024)
    mine = lax.dynamic_slice_in_dim(full, core * 128, 128, 0)
    other = lax.dynamic_slice_in_dim(full, (1 - core) * 128, 128, 0)

    def partials(rows):
        return jnp.concatenate(
            [
                dot(rows[:, :512], w_up, 1, 0).reshape(8, 16, 1024),
                dot(rows[:, 512:], w_down, 1, 1).reshape(8, 16, 1024),
            ],
            axis=1,
        )

    received = swap(partials(other))
    summed = (partials(mine) + received).astype(BF16)
    blocks = lax.all_to_all(summed, PLANE, 0, 0, tiled=True)
    total = jnp.sum(blocks.astype(F32), axis=0)
    hidden, grad_act = total[:16], total[16:]
    activated = gelu_tanh(hidden).astype(BF16)
    grad_hidden = gelu_back(hidden, grad_act)
    half = spread(jnp.concatenate([activated, grad_hidden], axis=0), PLANE, 8)
    half_other = swap(half)
    act = half[:, :16].reshape(128, 1024)
    grad = half[:, 16:].reshape(128, 1024)
    act_o = half_other[:, :16].reshape(128, 1024)
    grad_o = half_other[:, 16:].reshape(128, 1024)

    def outs(a, g):
        return jnp.concatenate([dot(a, w_down, 1, 0), dot(g, w_up, 1, 1)], axis=1).astype(BF16)

    out_mine = outs(act, grad)
    out_other = outs(act_o, grad_o)
    first = core == 0
    parts = jnp.concatenate(
        [jnp.where(first, out_mine, out_other), jnp.where(first, out_other, out_mine)], axis=0
    ).reshape(4, 64, 1024)
    near = jnp.sum(lax.all_to_all(parts, NEAR, 0, 0, tiled=True).astype(F32), axis=0)
    parts = near.astype(BF16).reshape(8, 8, 1024)
    sums = jnp.sum(lax.all_to_all(parts, FAR, 0, 0, tiled=True).astype(F32), axis=0).astype(BF16)

    both_a = jnp.concatenate([act, act_o], axis=0)
    both_g = jnp.concatenate([grad, grad_o], axis=0)
    rows = jnp.concatenate([mine, other], axis=0)
    grad_down = dot(both_a, rows[:, 512:], 0, 0).astype(BF16)
    grad_up = dot(rows[:, :512], both_g, 0, 0).astype(BF16)
    return (sums[:, :512], sums[:, 512:], grad_up, grad_down)


def solution(mesh):
    fine = Mesh(mesh.devices.reshape(SIZES), AXES)
    in_specs = (P(MP, DP), P(DP, MP), P(MP, DP), P(MP, DP))
    out_specs = (P(MP, DP), P(MP, DP), P(DP, MP), P(MP, DP))
    return jax.shard_map(local, mesh=fine, in_specs=in_specs, out_specs=out_specs, check_vma=False)
```

```python
import jax
import jax.numpy as jnp
from jax import lax
from jax.sharding import Mesh
from jax.sharding import PartitionSpec as P

AXES = ("zf", "zn", "yl", "x", "yh", "core")
SIZES = (8, 2, 2, 4, 2, 2)
MP = ("zf", "zn", "yl")
DP = ("x", "yh", "core")
FAR = "zf"
NEAR = ("zn", "yl")
PLANE = ("x", "yh")
F32 = jnp.float32
BF16 = jnp.bfloat16


def gelu_tanh(values):
    return (
        0.5
        * values
        * (1.0 + jnp.tanh(0.7978845608 * (values + 0.044715 * values * values * values)))
    )


def gelu_back(hidden, grad_act):
    unused, pullback = jax.vjp(gelu_tanh, hidden)
    return pullback(grad_act)[0].astype(BF16)


def dot(a, b, ca, cb):
    return lax.dot_general(a, b, (((ca,), (cb,)), ((), ())), preferred_element_type=F32)


def spread(block, axes, count):
    copies = jnp.broadcast_to(block[None], (count,) + block.shape)
    return lax.all_to_all(copies, axes, 0, 0, tiled=True)


def total(blocks):
    acc = blocks[0].astype(F32)
    for i in range(1, blocks.shape[0]):
        acc = acc + blocks[i].astype(F32)
    return acc


def swap(block):
    return lax.ppermute(block, "core", [(0, 1), (1, 0)])


def local(inputs, w_up, w_down, cotangent):
    core = lax.axis_index("core")
    pair = jnp.concatenate([inputs, cotangent], axis=1)
    far = spread(pair, FAR, 8).reshape(64, 1024)
    full = spread(far, NEAR, 4).reshape(256, 1024)
    mine = lax.dynamic_slice_in_dim(full, core * 128, 128, 0)
    other = lax.dynamic_slice_in_dim(full, (1 - core) * 128, 128, 0)

    def partials(rows):
        return jnp.concatenate(
            [
                dot(rows[:, :512], w_up, 1, 0).reshape(8, 16, 1024),
                dot(rows[:, 512:], w_down, 1, 1).reshape(8, 16, 1024),
            ],
            axis=1,
        )

    received = swap(partials(other).astype(BF16))
    summed = (partials(mine) + received).astype(BF16)
    blocks = lax.all_to_all(summed, PLANE, 0, 0, tiled=True)
    hidden, grad_act = total(blocks[:, :16]), total(blocks[:, 16:])
    activated = gelu_tanh(hidden).astype(BF16)
    grad_hidden = gelu_back(hidden, grad_act)
    half = spread(jnp.concatenate([activated, grad_hidden], axis=0), PLANE, 8)
    half_other = swap(half)
    act = half[:, :16].reshape(128, 1024)
    grad = half[:, 16:].reshape(128, 1024)
    act_o = half_other[:, :16].reshape(128, 1024)
    grad_o = half_other[:, 16:].reshape(128, 1024)

    def outs(a, g):
        return jnp.concatenate([dot(a, w_down, 1, 0), dot(g, w_up, 1, 1)], axis=1).astype(BF16)

    out_mine = outs(act, grad)
    out_other = outs(act_o, grad_o)
    first = core == 0
    parts = jnp.concatenate(
        [jnp.where(first, out_mine, out_other), jnp.where(first, out_other, out_mine)], axis=0
    ).reshape(4, 64, 1024)
    near = total(lax.all_to_all(parts, NEAR, 0, 0, tiled=True))
    parts = near.astype(BF16).reshape(8, 8, 1024)
    sums = total(lax.all_to_all(parts, FAR, 0, 0, tiled=True)).astype(BF16)

    both_a = jnp.concatenate([act, act_o], axis=0)
    both_g = jnp.concatenate([grad, grad_o], axis=0)
    rows = jnp.concatenate([mine, other], axis=0)
    grad_down = dot(both_a, rows[:, 512:], 0, 0).astype(BF16)
    grad_up = dot(rows[:, :512], both_g, 0, 0).astype(BF16)
    return (sums[:, :512], sums[:, 512:], grad_up, grad_down)


def solution(mesh):
    fine = Mesh(mesh.devices.reshape(SIZES), AXES)
    in_specs = (P(MP, DP), P(DP, MP), P(MP, DP), P(MP, DP))
    out_specs = (P(MP, DP), P(MP, DP), P(DP, MP), P(MP, DP))
    return jax.shard_map(local, mesh=fine, in_specs=in_specs, out_specs=out_specs, check_vma=False)
```

```python
import jax
import jax.numpy as jnp
from jax import lax
from jax.sharding import Mesh
from jax.sharding import PartitionSpec as P

AXES = ("zf", "zn", "yl", "x", "yh", "core")
SIZES = (8, 2, 2, 4, 2, 2)
MP = ("zf", "zn", "yl")
DP = ("x", "yh", "core")
FAR = "zf"
NEAR = ("zn", "yl")
PLANE = ("x", "yh")
ORDER = (5, 6, 7, 0, 1, 2, 3, 4)
F32 = jnp.float32
BF16 = jnp.bfloat16


def gelu_tanh(values):
    return (
        0.5
        * values
        * (1.0 + jnp.tanh(0.7978845608 * (values + 0.044715 * values * values * values)))
    )


def gelu_back(hidden, grad_act):
    unused, pullback = jax.vjp(gelu_tanh, hidden)
    return pullback(grad_act)[0].astype(BF16)


def dot(a, b, ca, cb):
    return lax.dot_general(a, b, (((ca,), (cb,)), ((), ())), preferred_element_type=F32)


def trade(chunks, axes, order=None):
    return lax.all_to_all(chunks, axes, 0, 0, axis_index_groups=order, tiled=True)


def spread(block, axes, count, order=None):
    return trade(jnp.broadcast_to(block[None], (count,) + block.shape), axes, order)


def total(blocks):
    acc = blocks[0].astype(F32)
    for i in range(1, blocks.shape[0]):
        acc = acc + blocks[i].astype(F32)
    return acc


def swap(block):
    return lax.ppermute(block, "core", [(0, 1), (1, 0)])


def local(inputs, w_up, w_down, cotangent):
    core = lax.axis_index("core")
    pair = jnp.concatenate([inputs, cotangent], axis=1)
    far = spread(pair, FAR, 8, [ORDER]).reshape(64, 1024)
    full = spread(far, NEAR, 4).reshape(256, 1024)
    mine = lax.dynamic_slice_in_dim(full, core * 128, 128, 0)
    other = lax.dynamic_slice_in_dim(full, (1 - core) * 128, 128, 0)

    def partials(rows):
        return jnp.concatenate(
            [
                dot(rows[:, :512], w_up, 1, 0).reshape(8, 16, 1024),
                dot(rows[:, 512:], w_down, 1, 1).reshape(8, 16, 1024),
            ],
            axis=1,
        )

    received = swap(partials(other).astype(BF16))
    summed = (partials(mine) + received).astype(BF16)
    blocks = trade(summed, PLANE)
    hidden, grad_act = total(blocks[:, :16]), total(blocks[:, 16:])
    activated = gelu_tanh(hidden).astype(BF16)
    grad_hidden = gelu_back(hidden, grad_act)
    half = spread(jnp.concatenate([activated, grad_hidden], axis=0), PLANE, 8)
    half_other = swap(half)
    act = half[:, :16].reshape(128, 1024)
    grad = half[:, 16:].reshape(128, 1024)
    act_o = half_other[:, :16].reshape(128, 1024)
    grad_o = half_other[:, 16:].reshape(128, 1024)

    def outs(a, g):
        return jnp.concatenate([dot(a, w_down, 1, 0), dot(g, w_up, 1, 1)], axis=1).astype(BF16)

    out_mine = outs(act, grad)
    out_other = outs(act_o, grad_o)
    first = core == 0
    parts = jnp.concatenate(
        [jnp.where(first, out_mine, out_other), jnp.where(first, out_other, out_mine)], axis=0
    ).reshape(4, 64, 1024)
    near = total(trade(parts, NEAR))
    parts = near.astype(BF16).reshape(8, 8, 1024)
    sums = total(trade(parts, FAR, [ORDER])).astype(BF16)

    both_a = jnp.concatenate([act, act_o], axis=0)
    both_g = jnp.concatenate([grad, grad_o], axis=0)
    rows = jnp.concatenate([mine, other], axis=0)
    grad_down = dot(both_a, rows[:, 512:], 0, 0).astype(BF16)
    grad_up = dot(rows[:, :512], both_g, 0, 0).astype(BF16)
    return (sums[:, :512], sums[:, 512:], grad_up, grad_down)


def solution(mesh):
    fine = Mesh(mesh.devices.reshape(SIZES), AXES)
    in_specs = (P(MP, DP), P(DP, MP), P(MP, DP), P(MP, DP))
    out_specs = (P(MP, DP), P(MP, DP), P(DP, MP), P(MP, DP))
    return jax.shard_map(local, mesh=fine, in_specs=in_specs, out_specs=out_specs, check_vma=False)
```

```python
import jax
import jax.numpy as jnp
from jax import lax
from jax.experimental import pallas as pl
from jax.experimental.pallas import tpu as pltpu
from jax.sharding import Mesh
from jax.sharding import PartitionSpec as P

AXES = ("zf", "zn", "yl", "x", "yh", "core")
SIZES = (8, 2, 2, 4, 2, 2)
MP = ("zf", "zn", "yl")
DP = ("x", "yh", "core")
FAR = "zf"
NEAR = ("zn", "yl")
PLANE = ("x", "yh")
ORDER = (5, 6, 7, 0, 1, 2, 3, 4)
F32 = jnp.float32
BF16 = jnp.bfloat16


def gelu_tanh(values):
    return (
        0.5
        * values
        * (1.0 + jnp.tanh(0.7978845608 * (values + 0.044715 * values * values * values)))
    )


def gelu_back(hidden, grad_act):
    unused, pullback = jax.vjp(gelu_tanh, hidden)
    return pullback(grad_act)[0].astype(BF16)


def dot(a, b, ca, cb):
    return lax.dot_general(a, b, (((ca,), (cb,)), ((), ())), preferred_element_type=F32)


def trade(chunks, axes, order=None):
    return lax.all_to_all(chunks, axes, 0, 0, axis_index_groups=order, tiled=True)


def spread(block, axes, count, order=None):
    return trade(jnp.broadcast_to(block[None], (count,) + block.shape), axes, order)


def total(blocks):
    acc = blocks[0].astype(F32)
    for i in range(1, blocks.shape[0]):
        acc = acc + blocks[i].astype(F32)
    return acc


def swap(block):
    return lax.ppermute(block, "core", [(0, 1), (1, 0)])


def call(body, shape, *args, dtype=BF16, after=()):
    shape = jax.tree.map(lambda s: pltpu.VMEM(s, dtype), shape, is_leaf=lambda s: isinstance(s[0], int))
    args = [pltpu.with_memory_space_constraint(a, pltpu.VMEM) for a in args]
    return pl.pallas_call(
        body,
        out_shape=shape,
        in_specs=[pl.BlockSpec(memory_space=pltpu.VMEM)] * len(args)
        + [pl.BlockSpec(memory_space=pl.ANY)] * len(after),
        out_specs=jax.tree.map(lambda s: pl.BlockSpec(memory_space=pltpu.VMEM), shape),
        compiler_params=pltpu.CompilerParams(vmem_limit_bytes=40 * 2**20),
    )(*args, *after)


def half_rows(ref, mine):
    core = lax.axis_index("core")
    start = pl.multiple_of((core if mine else 1 - core) * 128, 128)
    return ref[pl.ds(start, 128), :]


def partials(full, w_up, w_down, mine):
    rows = half_rows(full, mine)
    hidden = dot(rows[:, :512], w_up[...], 1, 0)
    grad_act = dot(rows[:, 512:], w_down[...], 1, 1)
    return hidden.reshape(8, 16, 1024), grad_act.reshape(8, 16, 1024)


def first_half(full, w_up, w_down, out):
    hidden, grad_act = partials(full, w_up, w_down, False)
    out[:, :16] = hidden.astype(BF16)
    out[:, 16:] = grad_act.astype(BF16)


def second_half(full, w_up, w_down, out):
    out[:, :16], out[:, 16:] = partials(full, w_up, w_down, True)


def add_received(mine, received, out):
    out[...] = (mine[...] + received[...].astype(F32)).astype(BF16)


def activate(blocks, out):
    hidden = total(blocks[:, :16])
    grad_act = total(blocks[:, 16:])
    cubic = 0.7978845608 * (hidden + 0.044715 * hidden * hidden * hidden)
    tanh = jnp.tanh(cubic)
    activated = (0.5 * hidden * (1.0 + tanh)).astype(BF16)
    slope = 0.7978845608 * (1.0 + 3 * 0.044715 * hidden * hidden)
    back = 0.5 * (1.0 + tanh) + 0.5 * hidden * (1.0 - tanh * tanh) * slope
    grad_hidden = (grad_act * back).astype(BF16)
    for i in range(8):
        out[i, :16] = activated
        out[i, 16:] = grad_hidden


def products(half, w_up, w_down):
    act = half[:, :16].reshape(128, 1024)
    grad = half[:, 16:].reshape(128, 1024)
    return dot(act, w_down[...], 1, 0).astype(BF16), dot(grad, w_up[...], 1, 1).astype(BF16)


def first_out(half, w_up, w_down, out):
    out[:, :512], out[:, 512:] = products(half, w_up, w_down)


def second_out(half, w_up, w_down, mine, out):
    core = lax.axis_index("core")
    other = pl.multiple_of((1 - core) * 128, 128)
    out[pl.ds(pl.multiple_of(core * 128, 128), 128), :] = mine[...]
    result, grad = products(half, w_up, w_down)
    out[pl.ds(other, 128), :512] = result
    out[pl.ds(other, 128), 512:] = grad


def add_four(blocks, out):
    out[...] = total(blocks).astype(BF16)


def repeat_four(block, out):
    for i in range(4):
        out[i] = block[...]


def align(full, half, half_other, after, act, grad, x, g):
    for i, part in enumerate((half, half_other)):
        act[128 * i : 128 * i + 128] = part[:, :16].reshape(128, 1024)
        grad[128 * i : 128 * i + 128] = part[:, 16:].reshape(128, 1024)
        rows = half_rows(full, i == 0)
        x[128 * i : 128 * i + 128] = rows[:, :512]
        g[128 * i : 128 * i + 128] = rows[:, 512:]


def local(inputs, w_up, w_down, cotangent):
    pair = jnp.concatenate([inputs, cotangent], axis=1)
    far = spread(pair, FAR, 8, [ORDER]).reshape(64, 1024)
    full = trade(call(repeat_four, (4, 64, 1024), far), NEAR).reshape(256, 1024)
    received = swap(call(first_half, (8, 32, 1024), full, w_up, w_down))
    own = call(second_half, (8, 32, 1024), full, w_up, w_down, dtype=F32)
    summed = call(add_received, (8, 32, 1024), own, received)
    half = trade(call(activate, (8, 32, 1024), trade(summed, PLANE)), PLANE)
    half_other = swap(half)
    mine = call(first_out, (128, 1024), half, w_up, w_down)
    parts = call(second_out, (256, 1024), half_other, w_up, w_down, mine).reshape(4, 64, 1024)
    near = call(add_four, (64, 1024), trade(parts, NEAR))
    sums = total(trade(near.reshape(8, 8, 1024), FAR, [ORDER])).astype(BF16)

    sizes = [(256, 1024), (256, 1024), (256, 512), (256, 512)]
    act, grad, x, g = call(align, sizes, full, half, half_other, after=(near,))
    grad_down = dot(act, g, 0, 0).astype(BF16)
    grad_up = dot(x, grad, 0, 0).astype(BF16)
    return (sums[:, :512], sums[:, 512:], grad_up, grad_down)


def solution(mesh):
    fine = Mesh(mesh.devices.reshape(SIZES), AXES)
    in_specs = (P(MP, DP), P(DP, MP), P(MP, DP), P(MP, DP))
    out_specs = (P(MP, DP), P(MP, DP), P(DP, MP), P(MP, DP))
    return jax.shard_map(local, mesh=fine, in_specs=in_specs, out_specs=out_specs, check_vma=False)
```

```python
import jax
import jax.numpy as jnp
from jax import lax
from jax.experimental import pallas as pl
from jax.experimental.pallas import tpu as pltpu
from jax.sharding import Mesh
from jax.sharding import PartitionSpec as P

AXES = ("zf", "zn", "yl", "x", "yh", "core")
SIZES = (8, 2, 2, 4, 2, 2)
MP = ("zf", "zn", "yl")
DP = ("x", "yh", "core")
FAR = "zf"
NEAR = ("zn", "yl")
ORDER = (5, 1, 6, 2, 7, 3, 0, 4)
PLANES = ("core", "x", "yh")
GROUPS = ((0, 4, 1, 5, 2, 6, 3, 7), (15, 14, 13, 12, 11, 10, 9, 8))
F32 = jnp.float32
BF16 = jnp.bfloat16


def gelu_tanh(values):
    return (
        0.5
        * values
        * (1.0 + jnp.tanh(0.7978845608 * (values + 0.044715 * values * values * values)))
    )


def gelu_back(hidden, grad_act):
    unused, pullback = jax.vjp(gelu_tanh, hidden)
    return pullback(grad_act)[0].astype(BF16)


def dot(a, b, ca, cb):
    return lax.dot_general(a, b, (((ca,), (cb,)), ((), ())), preferred_element_type=F32)


def trade(chunks, axes, order=None):
    return lax.all_to_all(chunks, axes, 0, 0, axis_index_groups=order, tiled=True)


def spread(block, axes, count, order=None):
    return trade(jnp.broadcast_to(block[None], (count,) + block.shape), axes, order)


def total(blocks):
    acc = blocks[0].astype(F32)
    for i in range(1, blocks.shape[0]):
        acc = acc + blocks[i].astype(F32)
    return acc


def swap(block):
    return lax.ppermute(block, "core", [(0, 1), (1, 0)])


def call(body, shape, *args, dtype=BF16, after=()):
    shape = jax.tree.map(lambda s: pltpu.VMEM(s, dtype), shape, is_leaf=lambda s: isinstance(s[0], int))
    args = [pltpu.with_memory_space_constraint(a, pltpu.VMEM) for a in args]
    return pl.pallas_call(
        body,
        out_shape=shape,
        in_specs=[pl.BlockSpec(memory_space=pltpu.VMEM)] * len(args)
        + [pl.BlockSpec(memory_space=pl.ANY)] * len(after),
        out_specs=jax.tree.map(lambda s: pl.BlockSpec(memory_space=pltpu.VMEM), shape),
        compiler_params=pltpu.CompilerParams(vmem_limit_bytes=40 * 2**20),
    )(*args, *after)


def half_rows(ref, mine):
    core = lax.axis_index("core")
    start = pl.multiple_of((core if mine else 1 - core) * 128, 128)
    return ref[pl.ds(start, 128), :]


def partials(full, w_up, w_down, mine):
    rows = half_rows(full, mine)
    hidden = dot(rows[:, :512], w_up[...], 1, 0)
    grad_act = dot(rows[:, 512:], w_down[...], 1, 1)
    return hidden.reshape(8, 16, 1024), grad_act.reshape(8, 16, 1024)


def first_half(full, w_up, w_down, out):
    hidden, grad_act = partials(full, w_up, w_down, False)
    out[:, :16] = hidden
    out[:, 16:] = grad_act


def second_half(full, w_up, w_down, out):
    out[:, :16], out[:, 16:] = partials(full, w_up, w_down, True)


def add_received(mine, received, out):
    out[...] = (mine[...] + received[...]).astype(BF16)


def activate(blocks, out):
    hidden = total(blocks[:, :16])
    grad_act = total(blocks[:, 16:])
    cubic = 0.7978845608 * (hidden + 0.044715 * hidden * hidden * hidden)
    tanh = jnp.tanh(cubic)
    activated = (0.5 * hidden * (1.0 + tanh)).astype(BF16)
    slope = 0.7978845608 * (1.0 + 3 * 0.044715 * hidden * hidden)
    back = 0.5 * (1.0 + tanh) + 0.5 * hidden * (1.0 - tanh * tanh) * slope
    grad_hidden = (grad_act * back).astype(BF16)
    for i in range(8):
        out[i, :16] = activated
        out[i, 16:] = grad_hidden


def products(half, w_up, w_down):
    act = half[:, :16].reshape(128, 1024)
    grad = half[:, 16:].reshape(128, 1024)
    return dot(act, w_down[...], 1, 0).astype(BF16), dot(grad, w_up[...], 1, 1).astype(BF16)


def first_out(half, w_up, w_down, out):
    out[:, :512], out[:, 512:] = products(half, w_up, w_down)


def second_out(half, w_up, w_down, mine, out):
    core = lax.axis_index("core")
    other = pl.multiple_of((1 - core) * 128, 128)
    out[pl.ds(pl.multiple_of(core * 128, 128), 128), :] = mine[...]
    result, grad = products(half, w_up, w_down)
    out[pl.ds(other, 128), :512] = result
    out[pl.ds(other, 128), 512:] = grad


def add_four(blocks, out):
    out[...] = total(blocks).astype(BF16)


def repeat_four(block, out):
    for i in range(4):
        out[i] = block[...]


def align(full, half, half_other, after, act, grad, x, g):
    for i, part in enumerate((half, half_other)):
        act[128 * i : 128 * i + 128] = part[:, :16].reshape(128, 1024)
        grad[128 * i : 128 * i + 128] = part[:, 16:].reshape(128, 1024)
        rows = half_rows(full, i == 0)
        x[128 * i : 128 * i + 128] = rows[:, :512]
        g[128 * i : 128 * i + 128] = rows[:, 512:]


def local(inputs, w_up, w_down, cotangent):
    pair = jnp.concatenate([inputs, cotangent], axis=1)
    far = spread(pair, FAR, 8, [ORDER]).reshape(64, 1024)
    full = trade(call(repeat_four, (4, 64, 1024), far), NEAR).reshape(256, 1024)
    received = swap(call(first_half, (8, 32, 1024), full, w_up, w_down, dtype=F32))
    own = call(second_half, (8, 32, 1024), full, w_up, w_down, dtype=F32)
    summed = call(add_received, (8, 32, 1024), own, received)
    half = trade(call(activate, (8, 32, 1024), trade(summed, PLANES, GROUPS)), PLANES, GROUPS)
    half_other = swap(half)
    mine = call(first_out, (128, 1024), half, w_up, w_down)
    parts = call(second_out, (256, 1024), half_other, w_up, w_down, mine).reshape(4, 64, 1024)
    near = call(add_four, (64, 1024), trade(parts, NEAR))
    sums = total(trade(near.reshape(8, 8, 1024), FAR, [ORDER])).astype(BF16)

    sizes = [(256, 1024), (256, 1024), (256, 512), (256, 512)]
    act, grad, x, g = call(align, sizes, full, half, half_other, after=(near,))
    grad_down = dot(act, g, 0, 0).astype(BF16)
    grad_up = dot(x, grad, 0, 0).astype(BF16)
    return (sums[:, :512], sums[:, 512:], grad_up, grad_down)


def solution(mesh):
    fine = Mesh(mesh.devices.reshape(SIZES), AXES)
    in_specs = (P(MP, DP), P(DP, MP), P(MP, DP), P(MP, DP))
    out_specs = (P(MP, DP), P(MP, DP), P(DP, MP), P(MP, DP))
    return jax.shard_map(local, mesh=fine, in_specs=in_specs, out_specs=out_specs, check_vma=False)
```

```python
import jax
import jax.numpy as jnp
from jax import lax
from jax.experimental import pallas as pl
from jax.experimental.pallas import tpu as pltpu
from jax.sharding import Mesh
from jax.sharding import PartitionSpec as P

AXES = ("zf", "zn", "yl", "x", "yh", "core")
SIZES = (8, 2, 2, 4, 2, 2)
MP = ("zf", "zn", "yl")
DP = ("x", "yh", "core")
FAR = "zf"
NEAR = ("zn", "yl")
ORDER = (5, 1, 6, 2, 7, 3, 0, 4)
PLANE = ("x", "yh")
PLANE_ORDER = (7, 3, 6, 2, 5, 1, 4, 0)
F32 = jnp.float32
BF16 = jnp.bfloat16


def gelu_tanh(values):
    return (
        0.5
        * values
        * (1.0 + jnp.tanh(0.7978845608 * (values + 0.044715 * values * values * values)))
    )


def gelu_back(hidden, grad_act):
    unused, pullback = jax.vjp(gelu_tanh, hidden)
    return pullback(grad_act)[0].astype(BF16)


def dot(a, b, ca, cb):
    return lax.dot_general(a, b, (((ca,), (cb,)), ((), ())), preferred_element_type=F32)


def trade(chunks, axes, order=None):
    return lax.all_to_all(chunks, axes, 0, 0, axis_index_groups=order, tiled=True)


def spread(block, axes, count, order=None):
    return trade(jnp.broadcast_to(block[None], (count,) + block.shape), axes, order)


def total(blocks):
    acc = blocks[0].astype(F32)
    for i in range(1, blocks.shape[0]):
        acc = acc + blocks[i].astype(F32)
    return acc


def swap(block):
    return lax.ppermute(block, "core", [(0, 1), (1, 0)])


def call(body, shape, *args, dtype=BF16, after=()):
    shape = jax.tree.map(lambda s: pltpu.VMEM(s, dtype), shape, is_leaf=lambda s: isinstance(s[0], int))
    args = [pltpu.with_memory_space_constraint(a, pltpu.VMEM) for a in args]
    return pl.pallas_call(
        body,
        out_shape=shape,
        in_specs=[pl.BlockSpec(memory_space=pltpu.VMEM)] * len(args)
        + [pl.BlockSpec(memory_space=pl.ANY)] * len(after),
        out_specs=jax.tree.map(lambda s: pl.BlockSpec(memory_space=pltpu.VMEM), shape),
        compiler_params=pltpu.CompilerParams(vmem_limit_bytes=40 * 2**20),
    )(*args, *after)


def half_rows(ref, mine):
    core = lax.axis_index("core")
    start = pl.multiple_of((core if mine else 1 - core) * 128, 128)
    return ref[pl.ds(start, 128), :]


def partials(full, w_up, w_down, mine):
    rows = half_rows(full, mine)
    hidden = dot(rows[:, :512], w_up[...], 1, 0)
    grad_act = dot(rows[:, 512:], w_down[...], 1, 1)
    return hidden.reshape(8, 16, 1024), grad_act.reshape(8, 16, 1024)


def first_half(full, w_up, w_down, out):
    hidden, grad_act = partials(full, w_up, w_down, False)
    out[:, :16] = hidden
    out[:, 16:] = grad_act


def second_half(full, w_up, w_down, out):
    out[:, :16], out[:, 16:] = partials(full, w_up, w_down, True)


def add_received(mine, received, out):
    out[...] = (mine[...] + received[...]).astype(BF16)


def activate(blocks, out):
    hidden = total(blocks[:, :16])
    grad_act = total(blocks[:, 16:])
    cubic = 0.7978845608 * (hidden + 0.044715 * hidden * hidden * hidden)
    tanh = jnp.tanh(cubic)
    activated = (0.5 * hidden * (1.0 + tanh)).astype(BF16)
    slope = 0.7978845608 * (1.0 + 3 * 0.044715 * hidden * hidden)
    back = 0.5 * (1.0 + tanh) + 0.5 * hidden * (1.0 - tanh * tanh) * slope
    grad_hidden = (grad_act * back).astype(BF16)
    for i in range(8):
        out[i, :16] = activated
        out[i, 16:] = grad_hidden


def products(half, w_up, w_down):
    act = half[:, :16].reshape(128, 1024)
    grad = half[:, 16:].reshape(128, 1024)
    return dot(act, w_down[...], 1, 0).astype(BF16), dot(grad, w_up[...], 1, 1).astype(BF16)


def first_out(half, w_up, w_down, out):
    out[:, :512], out[:, 512:] = products(half, w_up, w_down)


def second_out(half, w_up, w_down, mine, out):
    core = lax.axis_index("core")
    other = pl.multiple_of((1 - core) * 128, 128)
    out[pl.ds(pl.multiple_of(core * 128, 128), 128), :] = mine[...]
    result, grad = products(half, w_up, w_down)
    out[pl.ds(other, 128), :512] = result
    out[pl.ds(other, 128), 512:] = grad


def add_four(blocks, out):
    out[...] = total(blocks).astype(BF16)


def repeat_four(block, out):
    for i in range(4):
        out[i] = block[...]


def align(full, half, half_other, after, act, grad, x, g):
    for i, part in enumerate((half, half_other)):
        act[128 * i : 128 * i + 128] = part[:, :16].reshape(128, 1024)
        grad[128 * i : 128 * i + 128] = part[:, 16:].reshape(128, 1024)
        rows = half_rows(full, i == 0)
        x[128 * i : 128 * i + 128] = rows[:, :512]
        g[128 * i : 128 * i + 128] = rows[:, 512:]


def local(inputs, w_up, w_down, cotangent):
    pair = jnp.concatenate([inputs, cotangent], axis=1)
    far = spread(pair, FAR, 8, [ORDER]).reshape(64, 1024)
    full = trade(call(repeat_four, (4, 64, 1024), far), NEAR).reshape(256, 1024)
    received = swap(call(first_half, (8, 32, 1024), full, w_up, w_down, dtype=F32))
    own = call(second_half, (8, 32, 1024), full, w_up, w_down, dtype=F32)
    summed = call(add_received, (8, 32, 1024), own, received)
    half = trade(call(activate, (8, 32, 1024), trade(summed, PLANE, [PLANE_ORDER])), PLANE, [PLANE_ORDER])
    half_other = swap(half)
    mine = call(first_out, (128, 1024), half, w_up, w_down)
    parts = call(second_out, (256, 1024), half_other, w_up, w_down, mine).reshape(4, 64, 1024)
    near = call(add_four, (64, 1024), trade(parts, NEAR))
    sums = total(trade(near.reshape(8, 8, 1024), FAR, [ORDER])).astype(BF16)

    sizes = [(256, 1024), (256, 1024), (256, 512), (256, 512)]
    act, grad, x, g = call(align, sizes, full, half, half_other, after=(near,))
    grad_down = dot(act, g, 0, 0).astype(BF16)
    grad_up = dot(x, grad, 0, 0).astype(BF16)
    return (sums[:, :512], sums[:, 512:], grad_up, grad_down)


def solution(mesh):
    fine = Mesh(mesh.devices.reshape(SIZES), AXES)
    in_specs = (P(MP, DP), P(DP, MP), P(MP, DP), P(MP, DP))
    out_specs = (P(MP, DP), P(MP, DP), P(DP, MP), P(MP, DP))
    return jax.shard_map(local, mesh=fine, in_specs=in_specs, out_specs=out_specs, check_vma=False)
```

```python
import jax
import jax.numpy as jnp
from jax import lax
from jax.experimental import pallas as pl
from jax.experimental.pallas import tpu as pltpu
from jax.sharding import Mesh
from jax.sharding import PartitionSpec as P

AXES = ("zf", "zn", "yl", "x", "yh", "core")
SIZES = (8, 2, 2, 4, 2, 2)
MP = ("zf", "zn", "yl")
DP = ("x", "yh", "core")
FAR = "zf"
NEAR = ("zn", "yl")
ORDER = (5, 1, 6, 2, 7, 3, 0, 4)
PLANE = ("x", "yh")
PLANE_ORDER = (7, 3, 6, 2, 5, 1, 4, 0)
F32 = jnp.float32
BF16 = jnp.bfloat16


def gelu_tanh(values):
    return (
        0.5
        * values
        * (1.0 + jnp.tanh(0.7978845608 * (values + 0.044715 * values * values * values)))
    )


def gelu_back(hidden, grad_act):
    unused, pullback = jax.vjp(gelu_tanh, hidden)
    return pullback(grad_act)[0].astype(BF16)


def dot(a, b, ca, cb):
    return lax.dot_general(a, b, (((ca,), (cb,)), ((), ())), preferred_element_type=F32)


def trade(chunks, axes, order=None):
    return lax.all_to_all(chunks, axes, 0, 0, axis_index_groups=order, tiled=True)


def spread(block, axes, count, order=None):
    return trade(jnp.broadcast_to(block[None], (count,) + block.shape), axes, order)


def total(blocks):
    acc = blocks[0].astype(F32)
    for i in range(1, blocks.shape[0]):
        acc = acc + blocks[i].astype(F32)
    return acc


def swap(block):
    return lax.ppermute(block, "core", [(0, 1), (1, 0)])


def call(body, shape, *args, dtype=BF16, after=()):
    shape = jax.tree.map(lambda s: pltpu.VMEM(s, dtype), shape, is_leaf=lambda s: isinstance(s[0], int))
    args = [pltpu.with_memory_space_constraint(a, pltpu.VMEM) for a in args]
    return pl.pallas_call(
        body,
        out_shape=shape,
        in_specs=[pl.BlockSpec(memory_space=pltpu.VMEM)] * len(args)
        + [pl.BlockSpec(memory_space=pl.ANY)] * len(after),
        out_specs=jax.tree.map(lambda s: pl.BlockSpec(memory_space=pltpu.VMEM), shape),
        compiler_params=pltpu.CompilerParams(vmem_limit_bytes=40 * 2**20),
    )(*args, *after)


def half_rows(ref, mine):
    core = lax.axis_index("core")
    start = pl.multiple_of((core if mine else 1 - core) * 128, 128)
    return ref[pl.ds(start, 128), :]


def partials(full, w_up, w_down, mine):
    rows = half_rows(full, mine)
    hidden = dot(rows[:, :512], w_up[...], 1, 0)
    grad_act = dot(rows[:, 512:], w_down[...], 1, 1)
    return hidden.reshape(8, 16, 1024), grad_act.reshape(8, 16, 1024)


def first_half(full, w_up, w_down, out):
    hidden, grad_act = partials(full, w_up, w_down, False)
    out[:, :16] = hidden.astype(BF16)
    high = grad_act.astype(BF16)
    out[:, 16:32] = high
    out[:, 32:] = (grad_act - high.astype(F32)).astype(BF16)


def second_half(full, w_up, w_down, out):
    out[:, :16], out[:, 16:] = partials(full, w_up, w_down, True)


def add_received(mine, received, out):
    got = received[...].astype(F32)
    out[:, :16] = (mine[:, :16] + got[:, :16]).astype(BF16)
    out[:, 16:] = (mine[:, 16:] + (got[:, 16:32] + got[:, 32:])).astype(BF16)


def activate(blocks, out):
    hidden = total(blocks[:, :16])
    grad_act = total(blocks[:, 16:])
    cubic = 0.7978845608 * (hidden + 0.044715 * hidden * hidden * hidden)
    tanh = jnp.tanh(cubic)
    activated = (0.5 * hidden * (1.0 + tanh)).astype(BF16)
    slope = 0.7978845608 * (1.0 + 3 * 0.044715 * hidden * hidden)
    back = 0.5 * (1.0 + tanh) + 0.5 * hidden * (1.0 - tanh * tanh) * slope
    grad_hidden = (grad_act * back).astype(BF16)
    for i in range(8):
        out[i, :16] = activated
        out[i, 16:] = grad_hidden


def products(half, w_up, w_down):
    act = half[:, :16].reshape(128, 1024)
    grad = half[:, 16:].reshape(128, 1024)
    return dot(act, w_down[...], 1, 0).astype(BF16), dot(grad, w_up[...], 1, 1).astype(BF16)


def first_out(half, w_up, w_down, out):
    out[:, :512], out[:, 512:] = products(half, w_up, w_down)


def second_out(half, w_up, w_down, mine, out):
    core = lax.axis_index("core")
    other = pl.multiple_of((1 - core) * 128, 128)
    out[pl.ds(pl.multiple_of(core * 128, 128), 128), :] = mine[...]
    result, grad = products(half, w_up, w_down)
    out[pl.ds(other, 128), :512] = result
    out[pl.ds(other, 128), 512:] = grad


def add_four(blocks, out):
    out[...] = total(blocks).astype(BF16)


def repeat_four(block, out):
    for i in range(4):
        out[i] = block[...]


def align(full, half, half_other, after, act, grad, x, g):
    for i, part in enumerate((half, half_other)):
        act[128 * i : 128 * i + 128] = part[:, :16].reshape(128, 1024)
        grad[128 * i : 128 * i + 128] = part[:, 16:].reshape(128, 1024)
        rows = half_rows(full, i == 0)
        x[128 * i : 128 * i + 128] = rows[:, :512]
        g[128 * i : 128 * i + 128] = rows[:, 512:]


def local(inputs, w_up, w_down, cotangent):
    pair = jnp.concatenate([inputs, cotangent], axis=1)
    far = spread(pair, FAR, 8, [ORDER]).reshape(64, 1024)
    full = trade(call(repeat_four, (4, 64, 1024), far), NEAR).reshape(256, 1024)
    received = swap(call(first_half, (8, 48, 1024), full, w_up, w_down))
    own = call(second_half, (8, 32, 1024), full, w_up, w_down, dtype=F32)
    summed = call(add_received, (8, 32, 1024), own, received)
    half = trade(call(activate, (8, 32, 1024), trade(summed, PLANE, [PLANE_ORDER])), PLANE, [PLANE_ORDER])
    half_other = swap(half)
    mine = call(first_out, (128, 1024), half, w_up, w_down)
    parts = call(second_out, (256, 1024), half_other, w_up, w_down, mine).reshape(4, 64, 1024)
    near = call(add_four, (64, 1024), trade(parts, NEAR))
    sums = total(trade(near.reshape(8, 8, 1024), FAR, [ORDER])).astype(BF16)

    sizes = [(256, 1024), (256, 1024), (256, 512), (256, 512)]
    act, grad, x, g = call(align, sizes, full, half, half_other, after=(near,))
    grad_down = dot(act, g, 0, 0).astype(BF16)
    grad_up = dot(x, grad, 0, 0).astype(BF16)
    return (sums[:, :512], sums[:, 512:], grad_up, grad_down)


def solution(mesh):
    fine = Mesh(mesh.devices.reshape(SIZES), AXES)
    in_specs = (P(MP, DP), P(DP, MP), P(MP, DP), P(MP, DP))
    out_specs = (P(MP, DP), P(MP, DP), P(DP, MP), P(MP, DP))
    return jax.shard_map(local, mesh=fine, in_specs=in_specs, out_specs=out_specs, check_vma=False)
```

```python
import jax
import jax.numpy as jnp
from jax import lax
from jax.experimental import pallas as pl
from jax.experimental.pallas import tpu as pltpu
from jax.sharding import Mesh
from jax.sharding import PartitionSpec as P

AXES = ("zf", "zn", "yl", "x", "yh", "core")
SIZES = (8, 2, 2, 4, 2, 2)
MP = ("zf", "zn", "yl")
DP = ("x", "yh", "core")
FAR = "zf"
NEAR = ("zn", "yl")
NEAR_ORDER = (3, 2, 1, 0)
ORDER = (5, 1, 6, 2, 7, 3, 0, 4)
PLANE = ("x", "yh")
PLANE_ORDER = (7, 3, 6, 2, 5, 1, 4, 0)
F32 = jnp.float32
BF16 = jnp.bfloat16


def gelu_tanh(values):
    return (
        0.5
        * values
        * (1.0 + jnp.tanh(0.7978845608 * (values + 0.044715 * values * values * values)))
    )


def gelu_back(hidden, grad_act):
    unused, pullback = jax.vjp(gelu_tanh, hidden)
    return pullback(grad_act)[0].astype(BF16)


def dot(a, b, ca, cb):
    return lax.dot_general(a, b, (((ca,), (cb,)), ((), ())), preferred_element_type=F32)


def trade(chunks, axes, order=None):
    return lax.all_to_all(chunks, axes, 0, 0, axis_index_groups=order, tiled=True)


def spread(block, axes, count, order=None):
    return trade(jnp.broadcast_to(block[None], (count,) + block.shape), axes, order)


def total(blocks):
    acc = blocks[0].astype(F32)
    for i in range(1, blocks.shape[0]):
        acc = acc + blocks[i].astype(F32)
    return acc


def swap(block):
    return lax.ppermute(block, "core", [(0, 1), (1, 0)])


def call(body, shape, *args, dtype=BF16, after=()):
    shape = jax.tree.map(lambda s: pltpu.VMEM(s, dtype), shape, is_leaf=lambda s: isinstance(s[0], int))
    args = [pltpu.with_memory_space_constraint(a, pltpu.VMEM) for a in args]
    return pl.pallas_call(
        body,
        out_shape=shape,
        in_specs=[pl.BlockSpec(memory_space=pltpu.VMEM)] * len(args)
        + [pl.BlockSpec(memory_space=pl.ANY)] * len(after),
        out_specs=jax.tree.map(lambda s: pl.BlockSpec(memory_space=pltpu.VMEM), shape),
        compiler_params=pltpu.CompilerParams(vmem_limit_bytes=40 * 2**20),
    )(*args, *after)


def half_rows(ref, mine):
    core = lax.axis_index("core")
    start = pl.multiple_of((core if mine else 1 - core) * 128, 128)
    return ref[pl.ds(start, 128), :]


def partials(full, w_up, w_down, mine):
    rows = half_rows(full, mine)
    hidden = dot(rows[:, :512], w_up[...], 1, 0)
    grad_act = dot(rows[:, 512:], w_down[...], 1, 1)
    return hidden.reshape(8, 16, 1024), grad_act.reshape(8, 16, 1024)


def first_half(full, w_up, w_down, out):
    hidden, grad_act = partials(full, w_up, w_down, False)
    out[:, :16] = hidden
    out[:, 16:] = grad_act


def second_half(full, w_up, w_down, out):
    out[:, :16], out[:, 16:] = partials(full, w_up, w_down, True)


def add_received(mine, received, out):
    out[...] = (mine[...] + received[...]).astype(BF16)


def activate(blocks, out):
    hidden = total(blocks[:, :16])
    grad_act = total(blocks[:, 16:])
    cubic = 0.7978845608 * (hidden + 0.044715 * hidden * hidden * hidden)
    tanh = jnp.tanh(cubic)
    activated = (0.5 * hidden * (1.0 + tanh)).astype(BF16)
    slope = 0.7978845608 * (1.0 + 3 * 0.044715 * hidden * hidden)
    back = 0.5 * (1.0 + tanh) + 0.5 * hidden * (1.0 - tanh * tanh) * slope
    grad_hidden = (grad_act * back).astype(BF16)
    for i in range(8):
        out[i, :16] = activated
        out[i, 16:] = grad_hidden


def products(half, w_up, w_down):
    act = half[:, :16].reshape(128, 1024)
    grad = half[:, 16:].reshape(128, 1024)
    return dot(act, w_down[...], 1, 0).astype(BF16), dot(grad, w_up[...], 1, 1).astype(BF16)


def first_out(half, w_up, w_down, out):
    out[:, :512], out[:, 512:] = products(half, w_up, w_down)


def second_out(half, w_up, w_down, mine, out):
    core = lax.axis_index("core")
    other = pl.multiple_of((1 - core) * 128, 128)
    out[pl.ds(pl.multiple_of(core * 128, 128), 128), :] = mine[...]
    result, grad = products(half, w_up, w_down)
    out[pl.ds(other, 128), :512] = result
    out[pl.ds(other, 128), 512:] = grad


def add_four(blocks, out):
    out[...] = total(blocks).astype(BF16)


def repeat_four(block, out):
    for i in range(4):
        out[i] = block[...]


def align(full, half, half_other, after, act, grad, x, g):
    for i, part in enumerate((half, half_other)):
        act[128 * i : 128 * i + 128] = part[:, :16].reshape(128, 1024)
        grad[128 * i : 128 * i + 128] = part[:, 16:].reshape(128, 1024)
        rows = half_rows(full, i == 0)
        x[128 * i : 128 * i + 128] = rows[:, :512]
        g[128 * i : 128 * i + 128] = rows[:, 512:]


def local(inputs, w_up, w_down, cotangent):
    pair = jnp.concatenate([inputs, cotangent], axis=1)
    far = spread(pair, FAR, 8, [ORDER]).reshape(64, 1024)
    full = trade(call(repeat_four, (4, 64, 1024), far), NEAR, [NEAR_ORDER]).reshape(256, 1024)
    received = swap(call(first_half, (8, 32, 1024), full, w_up, w_down, dtype=F32))
    own = call(second_half, (8, 32, 1024), full, w_up, w_down, dtype=F32)
    summed = call(add_received, (8, 32, 1024), own, received)
    half = trade(call(activate, (8, 32, 1024), trade(summed, PLANE, [PLANE_ORDER])), PLANE, [PLANE_ORDER])
    half_other = swap(half)
    mine = call(first_out, (128, 1024), half, w_up, w_down)
    parts = call(second_out, (256, 1024), half_other, w_up, w_down, mine).reshape(4, 64, 1024)
    near = call(add_four, (64, 1024), trade(parts, NEAR, [NEAR_ORDER]))
    sums = total(trade(near.reshape(8, 8, 1024), FAR, [ORDER])).astype(BF16)

    sizes = [(256, 1024), (256, 1024), (256, 512), (256, 512)]
    act, grad, x, g = call(align, sizes, full, half, half_other, after=(near,))
    grad_down = dot(act, g, 0, 0).astype(BF16)
    grad_up = dot(x, grad, 0, 0).astype(BF16)
    return (sums[:, :512], sums[:, 512:], grad_up, grad_down)


def solution(mesh):
    fine = Mesh(mesh.devices.reshape(SIZES), AXES)
    in_specs = (P(MP, DP), P(DP, MP), P(MP, DP), P(MP, DP))
    out_specs = (P(MP, DP), P(MP, DP), P(DP, MP), P(MP, DP))
    return jax.shard_map(local, mesh=fine, in_specs=in_specs, out_specs=out_specs, check_vma=False)
```
